32 devices in a mesh: layer: 4 (over z), col: 4 (over x, core), row: 2 (over y).
Axes of the slice: x: 2, y: 2, z: 4, core: 2. Of those that a mesh axis runs over, the one named last changes fastest.
Arguments:
- front_copies: bfloat16 [4, 3072, 3072], P('layer', 'row', 'col'), may hold values from -6 to 6
- lower_panels: bfloat16 [4, 2, 3072, 512], P('layer', None, 'row', 'col'), may hold values from -0.25 to 0.25
- upper_panels: bfloat16 [4, 2, 512, 3072], P('layer', None, 'row', 'col'), may hold values from -6 to 6
- diag_blocks: float32 [4, 2, 512, 512], P('layer'), may hold values from -2 to 4, as said below
- block_fill: int32 [4, 2, 24], P('layer'), may hold values 0 or 1
- widths: int32 [4, 2], P('layer'), may hold values from 256 to 512, as said below
Outputs:
- summed_strips: float32 [4, 768, 3072], P('layer', 'row', 'col')
The draws below stay inside these ranges and needn't reach their ends.
Inputs may be any that keep to these rules, and one draw needn't show every extreme that they name: `widths`: each supernode uses between half and all of its 512 columns; some supernode uses all. `diag_blocks`: diagonal entries lie between 1 and 4.
All inputs are finite; a program needn't handle non-finite values. No bound on the sum of `block_fill` on one device may be relied on, other than what follows from the above.
Results may differ from the reference program's by a relative error of at most 0.0014.
Values may be sent and summed in bfloat16 or wider, within the bound.
A program may use at most 320 MiB of HBM per device.

```python
import math
import jax
import jax.numpy as jnp
from jax import lax

F = 3072
W = 512
S = 2
BLOCK = 128
NS_ITERS = 3
NB = 24
LAYERS = 4
GROUP = 4
N_ROW = 2


def draw_diag_blocks(key, part):
    key_diag = jax.random.fold_in(key, 11)
    key_off = jax.random.fold_in(key, 12)
    diagonal = jax.random.uniform(key_diag, (LAYERS, S, W), jnp.float32, 0.0, 1.0)
    diagonal = jnp.exp(diagonal * math.log(4.0))
    coupling = jnp.clip(jax.random.normal(key_off, (LAYERS, S, W, W), jnp.float32), -4.0, 4.0)
    scaling = jnp.sqrt(diagonal[:, :, :, None] * diagonal[:, :, None, :]) * (0.6 / math.sqrt(W))
    indices = jnp.arange(W, dtype=jnp.int32)
    off_diag = indices[:, None] != indices[None, :]
    return jnp.where(off_diag, coupling * scaling, diagonal[:, :, :, None] * jnp.ones((1, 1, 1, W), jnp.float32))


def draw_widths(key, part):
    values = jax.random.randint(jax.random.fold_in(key, 21), (LAYERS, S), W // 2, W + 1, jnp.int32)
    values = values.at[0, 0].set(W)
    return values.at[0, 1].set(W // 2)


def plant(entries, rng, low, top_value):
    longest = entries.shape.index(max(entries.shape))
    spots = []
    for shift in (0, 1):
        where = [jax.random.randint(jax.random.fold_in(rng, axis), (), 0, length) for axis, length in enumerate(entries.shape)]
        where[longest] = (where[longest] + shift) % entries.shape[longest]
        spots.append(tuple(where))
    return entries.at[spots[0]].set(low).at[spots[1]].set(top_value)


def steps_of(key, extent, shards, least, largest):
    def one(axis_at, blocks):
        heights = jax.random.uniform(jax.random.fold_in(jax.random.fold_in(key, 6), axis_at), (blocks,), jnp.float32, least / len(shards), largest / len(shards))
        return jnp.repeat(jnp.exp(heights), extent[axis_at] // blocks).reshape((-1,) + (1,) * (len(extent) - axis_at - 1))

    loudness = one(*shards[0])
    for cut in shards[1:]:
        loudness = loudness * one(*cut)
    return loudness


def scatter_about(own_key, extent, deviation, bound, split=(), held_as=jnp.bfloat16):
    gain = steps_of(own_key, extent, split, -0.22, 0.18) if split else 1.0
    values = jax.random.normal(own_key, extent, jnp.float32) * deviation * gain
    return jnp.minimum(jnp.maximum(values, -bound), bound).astype(held_as)


def setup_inputs(seed: int = 0) -> dict:
    keys = jax.random.split(jax.random.key(seed), 7)
    front_copies = scatter_about(keys[0], (LAYERS, F, F), 1.0, 6.0, ((0, 4), (1, 2), (2, 4)))
    lower_panels = scatter_about(keys[1], (LAYERS, S, F, W), W ** -0.5, 0.25, ((0, 4), (2, 2), (3, 4)))
    upper_panels = scatter_about(keys[2], (LAYERS, S, W, F), 1.0, 6.0, ((0, 4), (2, 2), (3, 4)))
    diag_blocks = draw_diag_blocks(jax.random.fold_in(keys[6], 71), 0)
    block_fill = plant((jax.random.randint(keys[4], (LAYERS, S, NB), 0, 3) < 2).astype(jnp.int32), jax.random.fold_in(keys[4], 1), 0, 1)
    widths = draw_widths(jax.random.fold_in(keys[6], 71), 0)
    return dict(front_copies=front_copies, lower_panels=lower_panels, upper_panels=upper_panels, diag_blocks=diag_blocks, block_fill=block_fill, widths=widths)


def masked_system(system_in, width_vec):
    order = system_in.shape[-1]
    indices = jnp.arange(order, dtype=jnp.int32)
    inside = indices[None, :] < width_vec[:, None]
    square = inside[:, :, None] & inside[:, None, :]
    identity = jnp.eye(order, dtype=system_in.dtype)
    return jnp.where(square, system_in, identity[None]), square


def schulz_inverse(system):
    diagonal = jnp.diagonal(system, axis1=1, axis2=2)
    order = system.shape[-1]
    current = jnp.eye(order, dtype=system.dtype)[None] / diagonal[:, None, :]
    for sweep_no in range(NS_ITERS):
        product = jnp.einsum("sij,sjk->sik", system, current, precision=lax.Precision.HIGHEST)
        current = 2.0 * current - jnp.einsum("sij,sjk->sik", current, product, precision=lax.Precision.HIGHEST)
    return current


def layer_update(front, lower, upper, system_in, width_vec, fill):
    system, square = masked_system(system_in, width_vec)
    inverse = schulz_inverse(system)
    kept_inverse = jnp.where(square, inverse, 0.0)
    fill_mask = jnp.repeat(fill, BLOCK, axis=1).astype(jnp.float32)
    scaled = jnp.einsum("sij,sjk->sik", kept_inverse, upper.astype(jnp.float32), precision=lax.Precision.HIGHEST)
    scaled_upper = (scaled * fill_mask[:, None, :]).astype(jnp.bfloat16)
    masked_lower = lower * fill_mask[:, :, None].astype(jnp.bfloat16)
    update = jnp.zeros((F, F), jnp.float32)
    for member in range(S):
        update = update + jnp.dot(masked_lower[member], scaled_upper[member], preferred_element_type=jnp.float32)
    return front.astype(jnp.float32) - update


def reference(front_copies, lower_panels, upper_panels, diag_blocks, block_fill, widths):
    def group_strips(group_no):
        first = group_no * GROUP

        def accumulate(total, offset):
            layer_no = (first + offset).astype(jnp.int32)
            front = lax.dynamic_index_in_dim(front_copies, layer_no, 0, keepdims=False)
            lower = lax.dynamic_index_in_dim(lower_panels, layer_no, 0, keepdims=False)
            upper = lax.dynamic_index_in_dim(upper_panels, layer_no, 0, keepdims=False)
            system_in = lax.dynamic_index_in_dim(diag_blocks, layer_no, 0, keepdims=False)
            fill = lax.dynamic_index_in_dim(block_fill, layer_no, 0, keepdims=False)
            width_vec = lax.dynamic_index_in_dim(widths, layer_no, 0, keepdims=False)
            return total + layer_update(front, lower, upper, system_in, width_vec, fill), None

        total, unused = lax.scan(accumulate, jnp.zeros((F, F), jnp.float32), jnp.arange(GROUP, dtype=jnp.int32))
        strips = total.reshape(N_ROW, GROUP, F // (GROUP * N_ROW), F)
        return jnp.transpose(strips, (1, 0, 2, 3)).reshape(GROUP, F // GROUP, F)

    result = lax.map(group_strips, jnp.arange(LAYERS // GROUP, dtype=jnp.int32))
    return result.reshape(LAYERS, F // GROUP, F)
```

```python
import functools

import jax
import jax.numpy as jnp
from jax import lax
from jax.experimental import pallas as pl
from jax.experimental.pallas import tpu as pltpu
from jax.sharding import PartitionSpec as P

BLOCK = 128
MESH = pl.DeviceIdType.MESH
CHUNK = 256
HEAD = 16


def pack(values, ref):
    rows, cols = values.shape
    top = jnp.maximum(jnp.max(jnp.abs(values), axis=0, keepdims=True), 1e-30)
    power = jnp.ceil(jnp.log2(top))
    coded = jnp.round(values * jnp.exp2(14.0 - power))
    ref[:HEAD, :] = jnp.broadcast_to(power, (HEAD, cols)).astype(jnp.int32).astype(jnp.int16)
    ref[HEAD:, :] = coded.astype(jnp.int32).astype(jnp.int16)


def unpack(ref):
    power = ref[:HEAD, :].astype(jnp.int32).astype(jnp.float32)[:1, :]
    coded = ref[HEAD:, :].astype(jnp.int32).astype(jnp.float32)
    return coded * jnp.exp2(power - 14.0)


def chain_kernel(n, strip, chunks, front, lower, upper, out, send, recv, send_sem, recv_sem):
    layer = lax.axis_index("layer")
    place = lax.rem(layer, n)
    base = layer - place
    has_left = place > 0
    has_right = place < n - 1
    barrier = pltpu.get_barrier_semaphore()

    @pl.when(has_left)
    def _():
        pl.semaphore_signal(barrier, inc=1, device_id={"layer": layer - 1}, device_id_type=MESH)

    @pl.when(has_right)
    def _():
        pl.semaphore_signal(barrier, inc=1, device_id={"layer": layer + 1}, device_id_type=MESH)

    pl.semaphore_wait(barrier, jnp.where(has_left, 1, 0) + jnp.where(has_right, 1, 0))

    members = lower.shape[0]

    def product(t, j):
        rows = pl.ds(pl.multiple_of(t * strip, strip), strip)
        cols = pl.ds(pl.multiple_of(j * CHUNK, CHUNK), CHUNK)
        total = front[rows, cols].astype(jnp.float32)
        for s in range(members):
            total = total - jnp.dot(
                lower[s, rows, :], upper[s, :, cols], preferred_element_type=jnp.float32
            )
        return total

    def copy(way, k, j, target):
        return pltpu.make_async_remote_copy(
            src_ref=send.at[way, k, j],
            dst_ref=recv.at[way, k, j],
            send_sem=send_sem.at[way, k, j],
            recv_sem=recv_sem.at[way, k, j],
            device_id={"layer": target},
            device_id_type=MESH,
        )

    first = jnp.where(place * 2 < n, 0, 1)

    def item(i, _):
        k, rest = i // (2 * chunks), i % (2 * chunks)
        j, turn = rest // 2, rest % 2
        way = jnp.where(turn == 0, first, 1 - first)
        t = jnp.where(way == 0, n - 1 - k, k)
        count = jnp.where(way == 0, n - 1 - place, place)
        fed = jnp.where(way == 0, place, n - 1 - place) > 0
        target = jnp.where(way == 0, layer + 1, layer - 1)
        source = jnp.where(way == 0, layer - 1, layer + 1)

        @pl.when(k < count)
        def _():
            value = product(t, j)
            slot = send.at[way, k, j]

            @pl.when(fed)
            def _():
                copy(way, k, j, source).wait_recv()
                pack(value + unpack(recv.at[way, k, j]), slot)

            @pl.when(jnp.logical_not(fed))
            def _():
                pack(value, slot)

            copy(way, k, j, target).start()

        return 0

    lax.fori_loop(0, (n - 1) * chunks * 2, item, 0)

    def own(j, _):
        cols = pl.ds(pl.multiple_of(j * CHUNK, CHUNK), CHUNK)
        out[0, :, cols] = product(place, j)
        return 0

    lax.fori_loop(0, chunks, own, 0)

    def finish(j, _):
        cols = pl.ds(pl.multiple_of(j * CHUNK, CHUNK), CHUNK)
        for turn in range(2):
            way = first if turn == 0 else 1 - first
            way = 1 - way
            k = jnp.where(way == 0, n - 1 - place, place)
            fed = jnp.where(way == 0, place, n - 1 - place) > 0
            source = jnp.where(way == 0, layer - 1, layer + 1)

            @pl.when(fed)
            def _():
                copy(way, k, j, source).wait_recv()
                out[0, :, cols] = out[0, :, cols] + unpack(recv.at[way, k, j])

        return 0

    lax.fori_loop(0, chunks, finish, 0)

    def drain(i, _):
        k, rest = i // (2 * chunks), i % (2 * chunks)
        j, way = rest // 2, rest % 2
        count = jnp.where(way == 0, n - 1 - place, place)
        target = jnp.where(way == 0, layer + 1, layer - 1)

        @pl.when(k < count)
        def _():
            copy(way, k, j, target).wait_send()

        return 0

    lax.fori_loop(0, (n - 1) * chunks * 2, drain, 0)


def update_and_sum(front, lower, upper, n):
    rows, cols = front.shape
    strip = rows // n
    chunks = cols // CHUNK
    return pl.pallas_call(
        functools.partial(chain_kernel, n, strip, chunks),
        out_shape=jax.ShapeDtypeStruct((1, strip, cols), jnp.float32),
        in_specs=[pl.BlockSpec(memory_space=pltpu.VMEM)] * 3,
        out_specs=pl.BlockSpec(memory_space=pltpu.VMEM),
        scratch_shapes=[
            pltpu.VMEM((2, n - 1, chunks, strip + HEAD, CHUNK), jnp.int16),
            pltpu.VMEM((2, n - 1, chunks, strip + HEAD, CHUNK), jnp.int16),
            pltpu.SemaphoreType.DMA((2, n - 1, chunks)),
            pltpu.SemaphoreType.DMA((2, n - 1, chunks)),
        ],
        compiler_params=pltpu.CompilerParams(
            collective_id=0, has_side_effects=True, vmem_limit_bytes=48 * 2**20
        ),
    )(front, lower, upper)


def kept_inverses(system_in, width_vec):
    order = system_in.shape[-1]
    indices = jnp.arange(order, dtype=jnp.int32)
    inside = indices[None, :] < width_vec[:, None]
    square = inside[:, :, None] & inside[:, None, :]
    eye = jnp.eye(order, dtype=jnp.float32)[None]
    system = jnp.where(square, system_in, eye)
    start = 1.0 / jnp.sum(system * eye, axis=2)
    inverse = 2.0 * eye * start[:, None, :] - start[:, :, None] * system * start[:, None, :]
    for _ in range(2):
        product = jnp.einsum("sij,sjk->sik", system, inverse, precision=lax.Precision.HIGH)
        inverse = 2.0 * inverse - jnp.einsum(
            "sij,sjk->sik", inverse, product, precision=lax.Precision.HIGH
        )
    return jnp.where(square, inverse, 0.0)


def on_device(front_copies, lower_panels, upper_panels, diag_blocks, block_fill, widths):
    front = front_copies[0]
    upper = upper_panels[0]
    row_count, col_count = front.shape
    fill_all = jnp.repeat(block_fill[0], BLOCK, axis=1).astype(jnp.float32)
    rows_mask = lax.dynamic_slice_in_dim(fill_all, lax.axis_index("row") * row_count, row_count, 1)
    cols_mask = lax.dynamic_slice_in_dim(fill_all, lax.axis_index("col") * col_count, col_count, 1)
    lower = lower_panels[0] * rows_mask[:, :, None].astype(jnp.bfloat16)
    lower = lax.all_gather(lower, "col", axis=2, tiled=True)
    upper = lax.all_gather(upper, "row", axis=1, tiled=True)
    inverse = kept_inverses(diag_blocks[0], widths[0])
    scaled = jnp.einsum(
        "sij,sjk->sik", inverse, upper.astype(jnp.float32), precision=lax.Precision.HIGH
    )
    scaled = (scaled * cols_mask[:, None, :]).astype(jnp.bfloat16)
    group = min(8, lax.axis_size("layer"))
    return update_and_sum(front, lower, scaled, group)


def solution(mesh):
    placed = (
        P("layer", "row", "col"),
        P("layer", None, "row", "col"),
        P("layer", None, "row", "col"),
        P("layer", None, None, None),
        P("layer", None, None),
        P("layer", None),
    )
    return jax.shard_map(
        on_device, mesh=mesh, in_specs=placed, out_specs=P("layer", "row", "col"), check_vma=False
    )
```

```python
import functools

import jax
import jax.numpy as jnp
from jax import lax
from jax.experimental import pallas as pl
from jax.experimental.pallas import tpu as pltpu
from jax.sharding import PartitionSpec as P

BLOCK = 128
MESH = pl.DeviceIdType.MESH
CHUNK = 256
HEAD = 16


def pack(values, ref):
    rows, cols = values.shape
    top = jnp.maximum(jnp.max(jnp.abs(values), axis=0, keepdims=True), 1e-30)
    power = jnp.ceil(jnp.log2(top))
    coded = jnp.round(values * jnp.exp2(14.0 - power))
    ref[:HEAD, :] = jnp.broadcast_to(power, (HEAD, cols)).astype(jnp.int32).astype(jnp.int16)
    ref[HEAD:, :] = coded.astype(jnp.int32).astype(jnp.int16)


def unpack(ref):
    power = ref[:HEAD, :].astype(jnp.int32).astype(jnp.float32)[:1, :]
    coded = ref[HEAD:, :].astype(jnp.int32).astype(jnp.float32)
    return coded * jnp.exp2(power - 14.0)


def split(values):
    high = values.astype(jnp.bfloat16)
    return high, (values - high.astype(jnp.float32)).astype(jnp.bfloat16)


def dot(a, b):
    return jnp.dot(a, b, preferred_element_type=jnp.float32)


def dot_split(a, b):
    return dot(a[0], b[0]) + (dot(a[0], b[1]) + dot(a[1], b[0]))


def inverse_of(block, width):
    rows = lax.broadcasted_iota(jnp.int32, block.shape, 0)
    cols = lax.broadcasted_iota(jnp.int32, block.shape, 1)
    square = (rows < width) & (cols < width)
    system = jnp.where(square, block, jnp.where(rows == cols, 1.0, 0.0))
    diagonal = jnp.where(rows == cols, system, 0.0)
    start_rows = 1.0 / jnp.sum(diagonal, axis=1, keepdims=True)
    start_cols = 1.0 / jnp.sum(diagonal, axis=0, keepdims=True)
    inverse = jnp.where(rows == cols, 2.0 * start_cols, 0.0) - start_rows * system * start_cols
    system = split(system)
    for _ in range(2):
        halves = split(inverse)
        product = split(dot_split(system, halves))
        inverse = 2.0 * inverse - dot_split(halves, product)
    return jnp.where(square, inverse, 0.0)


def front_kernel(
    n, n_col, n_row, strip, chunks,
    front_in, lower_in, upper_in, diag_in, fill, widths, out,
    front, lower_own, lower, upper, scaled, diag, inv, send, recv,
    load_sem, lower_send, lower_recv, upper_send, upper_recv, upper_load,
    inv_send, inv_recv, send_sem, recv_sem,
):
    layer = lax.axis_index("layer")
    col = lax.axis_index("col")
    row = lax.axis_index("row")
    place = lax.rem(layer, n)
    has_left = place > 0
    has_right = place < n - 1
    members, row_count, width = lower_own.shape
    part = upper_in.shape[2]
    half = lax.rem(col, 2)
    mate = col + 1 - 2 * half

    front_load = pltpu.make_async_copy(front_in.at[0], front, load_sem.at[0])
    lower_load = pltpu.make_async_copy(lower_in.at[0], lower_own, load_sem.at[1])
    diag_load = pltpu.make_async_copy(diag_in.at[0, half], diag, load_sem.at[2])
    lower_load.start()
    diag_load.start()

    def upper_view(ref_row, j):
        rows = pl.ds(pl.multiple_of(ref_row * part, part), part)
        return upper.at[:, rows, pl.ds(pl.multiple_of(j * CHUNK, CHUNK), CHUNK)]

    def upper_copy(d, j):
        return pltpu.make_async_remote_copy(
            src_ref=upper_in.at[0, :, :, pl.ds(pl.multiple_of(j * CHUNK, CHUNK), CHUNK)],
            dst_ref=upper_view(row, j),
            send_sem=upper_send.at[d - 1, j],
            recv_sem=upper_recv.at[d - 1, j],
            device_id={"row": lax.rem(row + d, n_row)},
            device_id_type=MESH,
        )

    def upper_arrived(d, j):
        return pltpu.make_async_remote_copy(
            src_ref=upper_in.at[0, :, :, pl.ds(pl.multiple_of(j * CHUNK, CHUNK), CHUNK)],
            dst_ref=upper_view(lax.rem(row + n_row - d, n_row), j),
            send_sem=upper_send.at[d - 1, j],
            recv_sem=upper_recv.at[d - 1, j],
            device_id={"row": lax.rem(row + n_row - d, n_row)},
            device_id_type=MESH,
        )

    rows_own = pl.ds(pl.multiple_of(row * part, part), part)
    upper_own = pltpu.make_async_copy(upper_in.at[0], upper.at[:, rows_own, :], upper_load)
    upper_own.start()
    front_load.start()

    barrier = pltpu.get_barrier_semaphore()

    @pl.when(has_left)
    def _():
        pl.semaphore_signal(barrier, inc=1, device_id={"layer": layer - 1}, device_id_type=MESH)

    @pl.when(has_right)
    def _():
        pl.semaphore_signal(barrier, inc=1, device_id={"layer": layer + 1}, device_id_type=MESH)

    for d in range(1, n_col):
        pl.semaphore_signal(
            barrier, inc=1, device_id={"col": lax.rem(col + d, n_col)}, device_id_type=MESH
        )
    for d in range(1, n_row):
        pl.semaphore_signal(
            barrier, inc=1, device_id={"row": lax.rem(row + d, n_row)}, device_id_type=MESH
        )
    near = jnp.where(has_left, 1, 0) + jnp.where(has_right, 1, 0)
    pl.semaphore_wait(barrier, near + n_col - 1 + n_row - 1)

    for j in range(chunks):
        for d in range(1, n_row):
            upper_copy(d, j).start()

    lower_load.wait()
    own_cols = pl.ds(pl.multiple_of(col * width, width), width)
    blocks = row_count // BLOCK
    for s in range(members):
        for b in range(blocks):
            flag = fill[0, s, row * blocks + b].astype(jnp.float32)
            piece = lower_own[s, b * BLOCK : (b + 1) * BLOCK, :].astype(jnp.float32) * flag
            lower[s, b * BLOCK : (b + 1) * BLOCK, own_cols] = piece.astype(jnp.bfloat16)

    def lower_copy(d, t, sign):
        peer = lax.rem(col + n_col + sign * d, n_col)
        source = col if sign > 0 else peer
        view = lower.at[
            :,
            pl.ds(pl.multiple_of(t * strip, strip), strip),
            pl.ds(pl.multiple_of(source * width, width), width),
        ]
        return pltpu.make_async_remote_copy(
            src_ref=view,
            dst_ref=view,
            send_sem=lower_send.at[d - 1, t],
            recv_sem=lower_recv.at[d - 1, t],
            device_id={"col": peer},
            device_id_type=MESH,
        )

    def send_strip(t):
        for d in range(1, n_col):
            lower_copy(d, t, 1).start()

    def send_strips(k, _):
        @pl.when(k < n - 1 - place)
        def _():
            send_strip(n - 1 - k)

        @pl.when(k < place)
        def _():
            send_strip(k)

        return 0

    lax.fori_loop(0, n - 1, send_strips, 0)
    send_strip(place)

    diag_load.wait()
    high, low = split(inverse_of(diag[...], widths[0, half]))
    inv[half, 0] = high
    inv[half, 1] = low

    def inv_copy(m):
        return pltpu.make_async_remote_copy(
            src_ref=inv.at[m],
            dst_ref=inv.at[m],
            send_sem=inv_send,
            recv_sem=inv_recv,
            device_id={"col": mate},
            device_id_type=MESH,
        )

    inv_copy(half).start()

    def scale(s, j):
        cols = pl.ds(pl.multiple_of(j * CHUNK, CHUNK), CHUNK)
        panel = upper[s, :, cols]
        value = dot(inv[s, 0], panel) + dot(inv[s, 1], panel)
        for b in range(CHUNK // BLOCK):
            flag = fill[0, s, (col * chunks + j) * (CHUNK // BLOCK) + b].astype(jnp.float32)
            piece = value[:, b * BLOCK : (b + 1) * BLOCK] * flag
            at = pl.ds(pl.multiple_of(j * CHUNK + b * BLOCK, BLOCK), BLOCK)
            scaled[s, :, at] = piece.astype(jnp.bfloat16)

    def wait_upper(j):
        for d in range(1, n_row):
            upper_arrived(d, j).wait_recv()

    def wait_lower(t):
        for d in range(1, n_col):
            lower_copy(d, t, -1).wait_recv()

    upper_own.wait()
    wait_upper(0)
    scale(half, 0)
    inv_copy(1 - half).wait_recv()
    scale(1 - half, 0)
    front_load.wait()

    def product(t, j):
        rows = pl.ds(pl.multiple_of(t * strip, strip), strip)
        cols = pl.ds(pl.multiple_of(j * CHUNK, CHUNK), CHUNK)
        total = front[rows, cols].astype(jnp.float32)
        for s in range(members):
            total = total - dot(lower[s, rows, :], scaled[s, :, cols])
        return total

    def copy(way, k, j, target):
        return pltpu.make_async_remote_copy(
            src_ref=send.at[way, k, j],
            dst_ref=recv.at[way, k, j],
            send_sem=send_sem.at[way, k, j],
            recv_sem=recv_sem.at[way, k, j],
            device_id={"layer": target},
            device_id_type=MESH,
        )

    first = jnp.where(place * 2 < n, 0, 1)

    def item(i, _):
        k, rest = i // (2 * chunks), i % (2 * chunks)
        j, turn = rest // 2, rest % 2
        way = jnp.where(turn == 0, first, 1 - first)
        t = jnp.where(way == 0, n - 1 - k, k)
        count = jnp.where(way == 0, n - 1 - place, place)
        fed = jnp.where(way == 0, place, n - 1 - place) > 0
        target = jnp.where(way == 0, layer + 1, layer - 1)
        source = jnp.where(way == 0, layer - 1, layer + 1)

        @pl.when((k == 0) & (j > 0) & (turn == 0))
        def _():
            wait_upper(j)
            for s in range(members):
                scale(s, j)

        @pl.when((k < count) & (j == 0))
        def _():
            wait_lower(t)

        @pl.when(k < count)
        def _():
            value = product(t, j)
            slot = send.at[way, k, j]

            @pl.when(fed)
            def _():
                copy(way, k, j, source).wait_recv()
                pack(value + unpack(recv.at[way, k, j]), slot)

            @pl.when(jnp.logical_not(fed))
            def _():
                pack(value, slot)

            copy(way, k, j, target).start()

        return 0

    lax.fori_loop(0, (n - 1) * chunks * 2, item, 0)

    wait_lower(place)

    def own(j, _):
        cols = pl.ds(pl.multiple_of(j * CHUNK, CHUNK), CHUNK)
        out[0, :, cols] = product(place, j)
        return 0

    lax.fori_loop(0, chunks, own, 0)

    def finish(j, _):
        cols = pl.ds(pl.multiple_of(j * CHUNK, CHUNK), CHUNK)
        for turn in range(2):
            way = first if turn == 0 else 1 - first
            way = 1 - way
            k = jnp.where(way == 0, n - 1 - place, place)
            fed = jnp.where(way == 0, place, n - 1 - place) > 0
            source = jnp.where(way == 0, layer - 1, layer + 1)

            @pl.when(fed)
            def _():
                copy(way, k, j, source).wait_recv()
                out[0, :, cols] = out[0, :, cols] + unpack(recv.at[way, k, j])

        return 0

    lax.fori_loop(0, chunks, finish, 0)

    def drain(i, _):
        k, rest = i // (2 * chunks), i % (2 * chunks)
        j, way = rest // 2, rest % 2
        count = jnp.where(way == 0, n - 1 - place, place)
        target = jnp.where(way == 0, layer + 1, layer - 1)

        @pl.when(k < count)
        def _():
            copy(way, k, j, target).wait_send()

        return 0

    lax.fori_loop(0, (n - 1) * chunks * 2, drain, 0)
    inv_copy(half).wait_send()
    for d in range(1, n_row):
        for j in range(chunks):
            upper_copy(d, j).wait_send()

    def drain_lower(t, _):
        for d in range(1, n_col):
            lower_copy(d, t, 1).wait_send()
        return 0

    lax.fori_loop(0, n, drain_lower, 0)


def on_device(n, n_col, n_row, front, lower, upper, diag, fill, widths):
    rows, cols = front.shape[1:]
    members, part = upper.shape[1:3]
    width = lower.shape[3]
    order = diag.shape[2]
    strip = rows // n
    chunks = cols // CHUNK
    anywhere = pl.BlockSpec(memory_space=pl.ANY)
    scalars = pl.BlockSpec(memory_space=pltpu.SMEM)
    dma = pltpu.SemaphoreType.DMA
    return pl.pallas_call(
        functools.partial(front_kernel, n, n_col, n_row, strip, chunks),
        out_shape=jax.ShapeDtypeStruct((1, strip, cols), jnp.float32),
        in_specs=[anywhere] * 4 + [scalars] * 2,
        out_specs=pl.BlockSpec(memory_space=pltpu.VMEM),
        scratch_shapes=[
            pltpu.VMEM((rows, cols), jnp.bfloat16),
            pltpu.VMEM((members, rows, width), jnp.bfloat16),
            pltpu.VMEM((members, rows, order), jnp.bfloat16),
            pltpu.VMEM((members, order, cols), jnp.bfloat16),
            pltpu.VMEM((members, order, cols), jnp.bfloat16),
            pltpu.VMEM((order, order), jnp.float32),
            pltpu.VMEM((members, 2, order, order), jnp.bfloat16),
            pltpu.VMEM((2, n - 1, chunks, strip + HEAD, CHUNK), jnp.int16),
            pltpu.VMEM((2, n - 1, chunks, strip + HEAD, CHUNK), jnp.int16),
            dma((3,)),
            dma((n_col - 1, n)),
            dma((n_col - 1, n)),
            dma((n_row - 1, chunks)),
            dma((n_row - 1, chunks)),
            dma,
            dma,
            dma,
            dma((2, n - 1, chunks)),
            dma((2, n - 1, chunks)),
        ],
        compiler_params=pltpu.CompilerParams(
            collective_id=0, has_side_effects=True, vmem_limit_bytes=48 * 2**20
        ),
    )(front, lower, upper, diag, fill, widths)


def solution(mesh):
    placed = (
        P("layer", "row", "col"),
        P("layer", None, "row", "col"),
        P("layer", None, "row", "col"),
        P("layer", None, None, None),
        P("layer", None, None),
        P("layer", None),
    )
    body = functools.partial(
        on_device, min(8, mesh.shape["layer"]), mesh.shape["col"], mesh.shape["row"]
    )
    return jax.shard_map(
        body, mesh=mesh, in_specs=placed, out_specs=P("layer", "row", "col"), check_vma=False
    )
```

```python
import functools

import jax
import jax.numpy as jnp
from jax import lax
from jax.experimental import pallas as pl
from jax.experimental.pallas import tpu as pltpu
from jax.sharding import PartitionSpec as P

BLOCK = 128
MESH = pl.DeviceIdType.MESH
CHUNK = 256


def pack(values, ref, scale):
    top = jnp.maximum(jnp.max(jnp.abs(values), axis=0, keepdims=True), 1e-30)
    power = jnp.ceil(jnp.log2(top))
    ref[...] = jnp.round(values * jnp.exp2(14.0 - power)).astype(jnp.int32).astype(jnp.int16)
    scale[...] = jnp.exp2(power - 14.0)


def unpack(ref, scale):
    return ref[...].astype(jnp.int32).astype(jnp.float32) * scale[...]


def split(values):
    high = values.astype(jnp.bfloat16)
    return high, (values - high.astype(jnp.float32)).astype(jnp.bfloat16)


def dot(a, b):
    return jnp.dot(a, b, preferred_element_type=jnp.float32)


def dot_split(a, b):
    return dot(a[0], b[0]) + (dot(a[0], b[1]) + dot(a[1], b[0]))


def inverse_of(block, width):
    rows = lax.broadcasted_iota(jnp.int32, block.shape, 0)
    cols = lax.broadcasted_iota(jnp.int32, block.shape, 1)
    square = (rows < width) & (cols < width)
    system = jnp.where(square, block, jnp.where(rows == cols, 1.0, 0.0))
    diagonal = jnp.where(rows == cols, system, 0.0)
    start_rows = 1.0 / jnp.sum(diagonal, axis=1, keepdims=True)
    start_cols = 1.0 / jnp.sum(diagonal, axis=0, keepdims=True)
    inverse = jnp.where(rows == cols, 2.0 * start_cols, 0.0) - start_rows * system * start_cols
    system = split(system)
    for _ in range(2):
        halves = split(inverse)
        product = split(dot_split(system, halves))
        inverse = 2.0 * inverse - dot_split(halves, product)
    return jnp.where(square, inverse, 0.0)


def front_kernel(
    n, n_col, n_row, strip, chunks,
    front_in, lower_in, upper_in, diag_in, fill, widths, out,
    front, lower_own, lower, upper, scaled, diag, inv, send, recv, send_scale, recv_scale,
    load_sem, lower_send, lower_recv, upper_send, upper_recv, upper_load,
    inv_send, inv_recv, send_sem, recv_sem, scale_send, scale_recv,
):
    layer = lax.axis_index("layer")
    col = lax.axis_index("col")
    row = lax.axis_index("row")
    place = lax.rem(layer, n)
    has_left = place > 0
    has_right = place < n - 1
    members, row_count, width = lower_own.shape
    part_rows = upper_in.shape[2]
    half = lax.rem(col, 2)
    mate = col + 1 - 2 * half

    front_load = pltpu.make_async_copy(front_in.at[0], front, load_sem.at[0])
    lower_load = pltpu.make_async_copy(lower_in.at[0], lower_own, load_sem.at[1])
    diag_load = pltpu.make_async_copy(diag_in.at[0, half], diag, load_sem.at[2])
    lower_load.start()
    diag_load.start()

    def upper_view(ref_row, j):
        rows = pl.ds(pl.multiple_of(ref_row * part_rows, part_rows), part_rows)
        return upper.at[:, rows, pl.ds(pl.multiple_of(j * CHUNK, CHUNK), CHUNK)]

    def upper_copy(d, j):
        return pltpu.make_async_remote_copy(
            src_ref=upper_in.at[0, :, :, pl.ds(pl.multiple_of(j * CHUNK, CHUNK), CHUNK)],
            dst_ref=upper_view(row, j),
            send_sem=upper_send.at[d - 1, j],
            recv_sem=upper_recv.at[d - 1, j],
            device_id={"row": lax.rem(row + d, n_row)},
            device_id_type=MESH,
        )

    def upper_arrived(d, j):
        return pltpu.make_async_remote_copy(
            src_ref=upper_in.at[0, :, :, pl.ds(pl.multiple_of(j * CHUNK, CHUNK), CHUNK)],
            dst_ref=upper_view(lax.rem(row + n_row - d, n_row), j),
            send_sem=upper_send.at[d - 1, j],
            recv_sem=upper_recv.at[d - 1, j],
            device_id={"row": lax.rem(row + n_row - d, n_row)},
            device_id_type=MESH,
        )

    rows_own = pl.ds(pl.multiple_of(row * part_rows, part_rows), part_rows)
    upper_own = pltpu.make_async_copy(upper_in.at[0], upper.at[:, rows_own, :], upper_load)
    upper_own.start()
    front_load.start()

    barrier = pltpu.get_barrier_semaphore()

    @pl.when(has_left)
    def _():
        pl.semaphore_signal(barrier, inc=1, device_id={"layer": layer - 1}, device_id_type=MESH)

    @pl.when(has_right)
    def _():
        pl.semaphore_signal(barrier, inc=1, device_id={"layer": layer + 1}, device_id_type=MESH)

    for d in range(1, n_col):
        pl.semaphore_signal(
            barrier, inc=1, device_id={"col": lax.rem(col + d, n_col)}, device_id_type=MESH
        )
    for d in range(1, n_row):
        pl.semaphore_signal(
            barrier, inc=1, device_id={"row": lax.rem(row + d, n_row)}, device_id_type=MESH
        )
    near = jnp.where(has_left, 1, 0) + jnp.where(has_right, 1, 0)
    pl.semaphore_wait(barrier, near + n_col - 1 + n_row - 1)

    for j in range(chunks):
        for d in range(1, n_row):
            upper_copy(d, j).start()

    lower_load.wait()
    own_cols = pl.ds(pl.multiple_of(col * width, width), width)
    blocks = row_count // BLOCK
    for s in range(members):
        for b in range(blocks):
            flag = fill[0, s, row * blocks + b].astype(jnp.float32)
            piece = lower_own[s, b * BLOCK : (b + 1) * BLOCK, :].astype(jnp.float32) * flag
            lower[s, b * BLOCK : (b + 1) * BLOCK, own_cols] = piece.astype(jnp.bfloat16)

    def lower_copy(d, t, sign):
        peer = lax.rem(col + n_col + sign * d, n_col)
        source = col if sign > 0 else peer
        view = lower.at[
            :,
            pl.ds(pl.multiple_of(t * strip, strip), strip),
            pl.ds(pl.multiple_of(source * width, width), width),
        ]
        return pltpu.make_async_remote_copy(
            src_ref=view,
            dst_ref=view,
            send_sem=lower_send.at[d - 1, t],
            recv_sem=lower_recv.at[d - 1, t],
            device_id={"col": peer},
            device_id_type=MESH,
        )

    def send_strip(t):
        for d in range(1, n_col):
            lower_copy(d, t, 1).start()

    def send_strips(k, _):
        @pl.when(k < n - 1 - place)
        def _():
            send_strip(n - 1 - k)

        @pl.when(k < place)
        def _():
            send_strip(k)

        return 0

    lax.fori_loop(0, n - 1, send_strips, 0)
    send_strip(place)

    diag_load.wait()
    high, low = split(inverse_of(diag[...], widths[0, half]))
    inv[half, 0] = high
    inv[half, 1] = low

    def inv_copy(m):
        return pltpu.make_async_remote_copy(
            src_ref=inv.at[m],
            dst_ref=inv.at[m],
            send_sem=inv_send,
            recv_sem=inv_recv,
            device_id={"col": mate},
            device_id_type=MESH,
        )

    inv_copy(half).start()

    def scale(s, j):
        cols = pl.ds(pl.multiple_of(j * CHUNK, CHUNK), CHUNK)
        panel = upper[s, :, cols]
        value = dot(inv[s, 0], panel) + dot(inv[s, 1], panel)
        for b in range(CHUNK // BLOCK):
            flag = fill[0, s, (col * chunks + j) * (CHUNK // BLOCK) + b].astype(jnp.float32)
            piece = value[:, b * BLOCK : (b + 1) * BLOCK] * flag
            at = pl.ds(pl.multiple_of(j * CHUNK + b * BLOCK, BLOCK), BLOCK)
            scaled[s, :, at] = piece.astype(jnp.bfloat16)

    def wait_upper(j):
        for d in range(1, n_row):
            upper_arrived(d, j).wait_recv()

    def wait_lower(t):
        for d in range(1, n_col):
            lower_copy(d, t, -1).wait_recv()

    upper_own.wait()
    wait_upper(0)
    scale(half, 0)
    inv_copy(1 - half).wait_recv()
    scale(1 - half, 0)
    front_load.wait()

    def product(t, j):
        rows = pl.ds(pl.multiple_of(t * strip, strip), strip)
        cols = pl.ds(pl.multiple_of(j * CHUNK, CHUNK), CHUNK)
        total = front[rows, cols].astype(jnp.float32)
        for s in range(members):
            total = total - dot(lower[s, rows, :], scaled[s, :, cols])
        return total

    def copies(way, k, j, target):
        parts = (
            (send_scale, recv_scale, scale_send, scale_recv),
            (send, recv, send_sem, recv_sem),
        )
        return [
            pltpu.make_async_remote_copy(
                src_ref=source.at[way, k, j],
                dst_ref=landing.at[way, k, j],
                send_sem=out_sem.at[way, k, j],
                recv_sem=in_sem.at[way, k, j],
                device_id={"layer": target},
                device_id_type=MESH,
            )
            for source, landing, out_sem, in_sem in parts
        ]

    first = jnp.where(place * 2 < n, 0, 1)

    def item(i, _):
        k, rest = i // (2 * chunks), i % (2 * chunks)
        j, turn = rest // 2, rest % 2
        way = jnp.where(turn == 0, first, 1 - first)
        t = jnp.where(way == 0, n - 1 - k, k)
        count = jnp.where(way == 0, n - 1 - place, place)
        fed = jnp.where(way == 0, place, n - 1 - place) > 0
        target = jnp.where(way == 0, layer + 1, layer - 1)
        source = jnp.where(way == 0, layer - 1, layer + 1)

        @pl.when((k == 0) & (j > 0) & (turn == 0))
        def _():
            wait_upper(j)
            for s in range(members):
                scale(s, j)

        @pl.when((k < count) & (j == 0))
        def _():
            wait_lower(t)

        @pl.when(k < count)
        def _():
            value = product(t, j)
            slot = send.at[way, k, j]

            @pl.when(fed)
            def _():
                for part in copies(way, k, j, source):
                    part.wait_recv()
                pack(
                    value + unpack(recv.at[way, k, j], recv_scale.at[way, k, j]),
                    slot,
                    send_scale.at[way, k, j],
                )

            @pl.when(jnp.logical_not(fed))
            def _():
                pack(value, slot, send_scale.at[way, k, j])

            for part in copies(way, k, j, target):
                part.start()

        return 0

    lax.fori_loop(0, (n - 1) * chunks * 2, item, 0)

    wait_lower(place)

    def own(j, _):
        cols = pl.ds(pl.multiple_of(j * CHUNK, CHUNK), CHUNK)
        out[0, :, cols] = product(place, j)
        return 0

    lax.fori_loop(0, chunks, own, 0)

    def finish(j, _):
        cols = pl.ds(pl.multiple_of(j * CHUNK, CHUNK), CHUNK)
        for turn in range(2):
            way = first if turn == 0 else 1 - first
            way = 1 - way
            k = jnp.where(way == 0, n - 1 - place, place)
            fed = jnp.where(way == 0, place, n - 1 - place) > 0
            source = jnp.where(way == 0, layer - 1, layer + 1)

            @pl.when(fed)
            def _():
                for part in copies(way, k, j, source):
                    part.wait_recv()
                out[0, :, cols] = out[0, :, cols] + unpack(
                    recv.at[way, k, j], recv_scale.at[way, k, j]
                )

        return 0

    lax.fori_loop(0, chunks, finish, 0)

    def drain(i, _):
        k, rest = i // (2 * chunks), i % (2 * chunks)
        j, way = rest // 2, rest % 2
        count = jnp.where(way == 0, n - 1 - place, place)
        target = jnp.where(way == 0, layer + 1, layer - 1)

        @pl.when(k < count)
        def _():
            for part in copies(way, k, j, target):
                part.wait_send()

        return 0

    lax.fori_loop(0, (n - 1) * chunks * 2, drain, 0)
    inv_copy(half).wait_send()
    for d in range(1, n_row):
        for j in range(chunks):
            upper_copy(d, j).wait_send()

    def drain_lower(t, _):
        for d in range(1, n_col):
            lower_copy(d, t, 1).wait_send()
        return 0

    lax.fori_loop(0, n, drain_lower, 0)


def on_device(n, n_col, n_row, front, lower, upper, diag, fill, widths):
    rows, cols = front.shape[1:]
    members, part = upper.shape[1:3]
    width = lower.shape[3]
    order = diag.shape[2]
    strip = rows // n
    chunks = cols // CHUNK
    anywhere = pl.BlockSpec(memory_space=pl.ANY)
    scalars = pl.BlockSpec(memory_space=pltpu.SMEM)
    dma = pltpu.SemaphoreType.DMA
    return pl.pallas_call(
        functools.partial(front_kernel, n, n_col, n_row, strip, chunks),
        out_shape=jax.ShapeDtypeStruct((1, strip, cols), jnp.float32),
        in_specs=[anywhere] * 4 + [scalars] * 2,
        out_specs=pl.BlockSpec(memory_space=pltpu.VMEM),
        scratch_shapes=[
            pltpu.VMEM((rows, cols), jnp.bfloat16),
            pltpu.VMEM((members, rows, width), jnp.bfloat16),
            pltpu.VMEM((members, rows, order), jnp.bfloat16),
            pltpu.VMEM((members, order, cols), jnp.bfloat16),
            pltpu.VMEM((members, order, cols), jnp.bfloat16),
            pltpu.VMEM((order, order), jnp.float32),
            pltpu.VMEM((members, 2, order, order), jnp.bfloat16),
            pltpu.VMEM((2, n - 1, chunks, strip, CHUNK), jnp.int16),
            pltpu.VMEM((2, n - 1, chunks, strip, CHUNK), jnp.int16),
            pltpu.VMEM((2, n - 1, chunks, 1, CHUNK), jnp.float32),
            pltpu.VMEM((2, n - 1, chunks, 1, CHUNK), jnp.float32),
            dma((3,)),
            dma((n_col - 1, n)),
            dma((n_col - 1, n)),
            dma((n_row - 1, chunks)),
            dma((n_row - 1, chunks)),
            dma,
            dma,
            dma,
            dma((2, n - 1, chunks)),
            dma((2, n - 1, chunks)),
            dma((2, n - 1, chunks)),
            dma((2, n - 1, chunks)),
        ],
        compiler_params=pltpu.CompilerParams(
            collective_id=0, has_side_effects=True, vmem_limit_bytes=60 * 2**20
        ),
    )(front, lower, upper, diag, fill, widths)


def solution(mesh):
    placed = (
        P("layer", "row", "col"),
        P("layer", None, "row", "col"),
        P("layer", None, "row", "col"),
        P("layer", None, None, None),
        P("layer", None, None),
        P("layer", None),
    )
    body = functools.partial(
        on_device, min(8, mesh.shape["layer"]), mesh.shape["col"], mesh.shape["row"]
    )
    return jax.shard_map(
        body, mesh=mesh, in_specs=placed, out_specs=P("layer", "row", "col"), check_vma=False
    )
```
